32 devices in a mesh: row: 4 (over y, core), col: 4 (over z), depth: 2 (over x).
Axes of the slice: x: 2, y: 2, z: 4, core: 2. Of those that a mesh axis runs over, the one named last changes fastest.
Arguments:
- covariance: float32 [7168, 7168], P('row', 'col'), may hold values from -1 to 5, as said below
- iterate: float32 [7168, 7168], P('row', 'col'), may hold values from -1 to 1.5
Outputs:
- refreshed: float32 [7168, 4096], P(('row', 'depth'), 'col')
The draws below stay inside these ranges and needn't reach their ends.
Inputs may be any that keep to these rules, and one draw needn't show every extreme that they name: `covariance`: symmetric.
All inputs are finite; a program needn't handle non-finite values.
Results may differ from the reference program's by a relative error of at most 0.00008.
Values sent between devices are 32-bit elements; how exact they have to be, the bound alone decides.
A program may use at most 128 MiB of HBM per device.

```python
import math
import jax
import jax.numpy as jnp
from jax import lax

N = 7168
PERIOD = 896
SLAB = 512
WINDOW = 4096


def diagonal_values(key):
    key = jax.random.fold_in(key, 11)
    logs = jax.random.uniform(key, (N,), jnp.float32, 0.0, math.log(4.0))
    return jnp.exp(logs)


def symmetric_noise(noise, scale):
    return (noise + noise.T) * (0.7071068 * scale / math.sqrt(N))


def draw_covariance(key, part):
    damped = diagonal_values(key)
    key = jax.random.fold_in(key, 3)
    noise = jax.random.truncated_normal(key, -6.0, 6.0, (N, N), jnp.float32)
    return symmetric_noise(noise, 0.25) + jnp.diag(damped)


def draw_iterate(key, part):
    damped = diagonal_values(key)
    key = jax.random.fold_in(key, 5)
    noise = jax.random.truncated_normal(key, -6.0, 6.0, (N, N), jnp.float32)
    return noise * (0.05 / math.sqrt(N)) + jnp.diag(1.0 / damped)


def setup_inputs(seed: int = 0) -> dict:
    keys = jax.random.split(jax.random.key(seed), 3)
    covariance = draw_covariance(jax.random.fold_in(keys[2], 71), 0)
    iterate = draw_iterate(jax.random.fold_in(keys[2], 71), 0)
    return {"covariance": covariance, "iterate": iterate}


def reference(covariance, iterate):
    positions = jnp.arange(WINDOW, dtype=jnp.int32)
    window = (positions // SLAB) * PERIOD + positions % SLAB
    window_cols = jnp.take(iterate, window, axis=1)
    product = jnp.dot(covariance, window_cols, precision=lax.Precision.HIGHEST, preferred_element_type=jnp.float32)
    indices = jnp.arange(N, dtype=jnp.int32)
    select = (indices[:, None] == window[None, :]).astype(jnp.float32)
    residual = 2.0 * select - product
    return jnp.dot(iterate, residual, precision=lax.Precision.HIGHEST, preferred_element_type=jnp.float32)
```

```python
import jax
import jax.numpy as jnp
from jax import lax
from jax.sharding import PartitionSpec as P

PERIOD = 896
SLAB = 512
CHUNK = 64
HIGH = lax.Precision.HIGH


def column_of(offset):
    return offset // SLAB * PERIOD + offset % SLAB


def halves(pick_second, array, axis):
    first, second = jnp.split(array, 2, axis=axis)
    return jnp.where(pick_second, second, first), jnp.where(pick_second, first, second)


def gather_line(block, size):
    right, left = [block], [block]
    for step in range(size - 1):
        right.append(
            lax.ppermute(right[-1], "col", [(i, i + 1) for i in range(step, size - 1)])
        )
        left.append(
            lax.ppermute(left[-1], "col", [(i + 1, i) for i in range(size - 1 - step)])
        )
    slots = [block]
    for slot in range(1, size):
        slots.append(left[slot] + right[size - slot])
    return jnp.concatenate(slots, axis=0)


def sum_rows(part, size):
    core = lax.axis_index("row") % 2
    kept, given = halves(core == 1, part, 0)
    cores = [(i, i ^ 1) for i in range(size)]
    kept = kept + lax.ppermute(given, "row", cores)
    bit = 2
    while bit < size:
        kept = kept + lax.ppermute(kept, "row", [(i, i ^ bit) for i in range(size)])
        bit *= 2
    other = lax.ppermute(kept, "row", cores)
    return jnp.where(
        core == 0,
        jnp.concatenate([kept, other], axis=0),
        jnp.concatenate([other, kept], axis=0),
    )


def scatter_line(part, size):
    slots = jnp.split(part, size, axis=0)
    right, left = None, None
    for step in range(size - 1):
        ahead = slots[size - 1 - step]
        behind = slots[step + 1]
        ahead = ahead if right is None else ahead + right
        behind = behind if left is None else behind + left
        right = lax.ppermute(ahead, "col", [(i, i + 1) for i in range(step + 1)])
        left = lax.ppermute(behind, "col", [(size - 1 - i, size - 2 - i) for i in range(step + 1)])
    return slots[0] + right + left


def solution(mesh):
    rows, cols = mesh.shape["row"], mesh.shape["col"]

    def local(covariance, iterate):
        tile_cols = covariance.shape[1]
        half = tile_cols // PERIOD * SLAB // 2
        chunk = min(CHUNK, half)
        depth = lax.axis_index("depth")
        own, peer = [], []
        gathered = []
        for start in range(0, half, chunk):
            near, far = column_of(start), column_of(half + start)
            window = jnp.where(
                depth == 0, iterate[:, near : near + chunk], iterate[:, far : far + chunk]
            ).T
            gathered.append(gather_line(window, cols))
        for number, start in enumerate(range(0, half, chunk)):
            near, far = column_of(start), column_of(half + start)
            part = jnp.dot(
                gathered[number],
                covariance,
                precision=HIGH,
                preferred_element_type=jnp.float32,
            )
            product = sum_rows(part, rows)
            here = jnp.where(depth == 0, near, far)
            shape = product.shape
            slot_row = lax.broadcasted_iota(jnp.int32, shape, 0)
            place = lax.broadcasted_iota(jnp.int32, shape, 1)
            select = (slot_row < chunk) & (place == here + slot_row)
            residual = jnp.where(select, 2.0, 0.0) - product
            part = lax.dot_general(
                residual,
                iterate,
                (((1,), (1,)), ((), ())),
                precision=HIGH,
                preferred_element_type=jnp.float32,
            )
            result = scatter_line(part, cols)
            kept, given = halves(depth == 1, result, 1)
            own.append(kept)
            peer.append(lax.ppermute(given, "depth", [(0, 1), (1, 0)]))
        first = jnp.where(depth == 0, jnp.concatenate(own, 0), jnp.concatenate(peer, 0))
        second = jnp.where(depth == 0, jnp.concatenate(peer, 0), jnp.concatenate(own, 0))
        return jnp.concatenate([first, second], axis=0).T

    in_specs = (P("row", "col"), P("row", "col"))
    out_specs = P(("row", "depth"), "col")
    return jax.shard_map(local, mesh=mesh, in_specs=in_specs, out_specs=out_specs, check_vma=False)
```

```python
import functools

import jax
import jax.numpy as jnp
from jax import lax
from jax.experimental import pallas as pl
from jax.experimental.pallas import tpu as pltpu
from jax.sharding import PartitionSpec as P

PERIOD = 896
SLAB = 512
CHUNK = 64
STRIP = 16
MESH = pl.DeviceIdType.MESH


def column_of(offset):
    return offset // SLAB * PERIOD + offset % SLAB


def tile_of(size):
    return 256 if size % 256 == 0 else 128 if size % 128 == 0 else size


def split(value):
    hi = value.astype(jnp.bfloat16)
    return hi, (value - hi.astype(jnp.float32)).astype(jnp.bfloat16)


def product3(hi, lo, other, contract):
    b_hi, b_lo = split(other)
    dot = functools.partial(
        lax.dot_general,
        dimension_numbers=(contract, ((), ())),
        preferred_element_type=jnp.float32,
    )
    return dot(hi, b_hi) + (dot(lo, b_hi) + dot(hi, b_lo))


def strips(rows, body):
    def step(i, carry):
        body(pl.multiple_of(i * STRIP, STRIP))
        return carry

    lax.fori_loop(0, rows // STRIP, step, 0)


def kernel(
    dims, w, a_hbm, x_hbm, out, a, x, ag, hi, lo, prod, core_in, bit_in, core_back, part, rs,
    keep, give, load_sem, own_sem, ag_send, ag_recv, core_send, core_recv, bit_send, bit_recv,
    back_send, back_recv, rs_send, rs_recv, give_send, give_recv, keep_sem,
):
    row_count, z, chunk, chunks, ring, rs_ring = dims
    row, col, depth = (lax.axis_index(n) for n in ("row", "col", "depth"))
    core = row % 2
    bits = [b for b in (2, 4, 8, 16, 32) if b < row_count]
    half = chunk * chunks
    group = z * chunk
    share = group // 2
    k_size, i_size = a.shape
    r_half = x.shape[0] // 2

    def partner(bit):
        return {"row": row + bit - 2 * bit * ((row // bit) % 2)}

    places = (col, z - 1 - col)
    targets = ({"col": col + 1}, {"col": col - 1})

    load_a = pltpu.make_async_copy(a_hbm, a, load_sem.at[0])
    load_x = pltpu.make_async_copy(x_hbm, x, load_sem.at[1])
    load_a.start()
    load_x.start()

    barrier = pltpu.get_barrier_semaphore()
    fixed = [partner(b) for b in [1] + bits] + [{"depth": 1 - depth}]
    for who in fixed:
        pl.semaphore_signal(barrier, inc=1, device_id=who, device_id_type=MESH)
    for way in range(2):

        @pl.when(places[way] < z - 1)
        def _():
            pl.semaphore_signal(barrier, inc=1, device_id=targets[way], device_id_type=MESH)

    ends = jnp.where(col == 0, 1, 0) + jnp.where(col == z - 1, 1, 0)
    pl.semaphore_wait(barrier, len(fixed) + 2 - ends)

    def remote(src, dst, send, recv, who):
        return pltpu.make_async_remote_copy(
            src_ref=src, dst_ref=dst, send_sem=send, recv_sem=recv,
            device_id=who, device_id_type=MESH,
        )

    def own_copy(c):
        return pltpu.make_async_copy(
            w.at[pl.ds(c * chunk, chunk)], ag.at[c % ring, 0], own_sem.at[c % ring]
        )

    def ag_copy(way, s, c):
        slot = c % ring
        came, lands = (z - s, z - 1 - s) if way == 0 else (s, s + 1)
        src = w.at[pl.ds(c * chunk, chunk)] if s == 0 else ag.at[slot, came]
        return remote(
            src, ag.at[slot, lands], ag_send.at[way, s, slot], ag_recv.at[way, s, slot],
            targets[way],
        )

    def rs_copy(way, s, c):
        slot = c % rs_ring
        src = part.at[c % z, z - 1 if way == 0 else 1] if s == 0 else rs.at[slot, way, s - 1]
        return remote(
            src, rs.at[slot, way, s], rs_send.at[way, s, slot], rs_recv.at[way, s, slot],
            targets[way],
        )

    mine = pl.ds(pl.multiple_of(core * share, share), share)
    theirs = pl.ds(pl.multiple_of((1 - core) * share, share), share)

    def core_copy(c):
        p = c % 2
        return remote(
            prod.at[p, theirs], core_in.at[p], core_send.at[p], core_recv.at[p], partner(1)
        )

    def back_copy(c):
        p = c % 2
        return remote(
            prod.at[p, mine], core_back.at[p], back_send.at[p], back_recv.at[p], partner(1)
        )

    def bit_copy(n, c):
        p = c % 2
        return remote(
            prod.at[p, mine], bit_in.at[n, p], bit_send.at[n, p], bit_recv.at[n, p],
            partner(bits[n]),
        )

    def give_copy(c):
        return remote(
            give.at[c % 2], out.at[pl.ds(depth * half + c * chunk, chunk)],
            give_send.at[c], give_recv.at[c], {"depth": 1 - depth},
        )

    def keep_copy(c):
        return pltpu.make_async_copy(
            keep.at[c % 2], out.at[pl.ds(depth * half + c * chunk, chunk)], keep_sem.at[c]
        )

    def live(c):
        return (c >= 0) & (c < chunks)

    def add_into_kept(p, other):
        base = core * share

        def body(r):
            at = pl.ds(pl.multiple_of(base + r, STRIP), STRIP)
            prod[p, at] = prod[p, at] + other[pl.ds(r, STRIP)]

        strips(share, body)

    def step(t, carry):
        for s in range(z - 1):
            c = t - 1 - s
            for way in range(2):
                place = places[way]

                @pl.when(live(c) & (place >= s + 1))
                def _():
                    ag_copy(way, s, c).wait_recv()

                @pl.when(live(c) & (place >= s) & (place < z - 1))
                def _():
                    ag_copy(way, s, c).wait_send()

        @pl.when(live(t - 1))
        def _():
            own_copy(t - 1).wait()

        for s in range(z - 1):
            c = t - 1 - z - s
            for way in range(2):
                place = places[way]

                @pl.when(live(c) & (place >= 1) & (place <= s + 1))
                def _():
                    rs_copy(way, s, c).wait_recv()

                @pl.when(live(c) & (place <= s) & (place < z - 1))
                def _():
                    rs_copy(way, s, c).wait_send()

        for s in range(z - 1):
            c = t - s
            for way in range(2):

                @pl.when(live(c) & (places[way] >= s) & (places[way] < z - 1))
                def _():
                    ag_copy(way, s, c).start()

        @pl.when(live(t))
        def _():
            own_copy(t).start()

        for s in range(1, z - 1):
            c = t - z - s
            for way in range(2):
                place = places[way]
                slot = c % rs_ring
                term = part.at[c % z, z - 1 - s if way == 0 else s + 1]
                sum_ref = rs.at[slot, way, s - 1]

                @pl.when(live(c) & (place >= 1) & (place <= s) & (place < z - 1))
                def _():
                    def body(r):
                        at = pl.ds(r, STRIP)
                        sum_ref[at] = sum_ref[at] + term[at]

                    strips(chunk, body)

                @pl.when(live(c) & (place == 0))
                def _():
                    def body(r):
                        at = pl.ds(r, STRIP)
                        sum_ref[at] = term[at]

                    strips(chunk, body)

                @pl.when(live(c) & (place <= s) & (place < z - 1))
                def _():
                    rs_copy(way, s, c).start()

        last = t - (2 * z - 1)

        @pl.when(live(last))
        def _():
            total = part.at[last % z, 0]
            for way in range(2):

                @pl.when(places[way] > 0)
                def _():
                    def body(r):
                        at = pl.ds(r, STRIP)
                        total[at] = total[at] + rs[last % rs_ring, way, z - 2, at]

                    strips(chunk, body)

            @pl.when(last >= 2)
            def _():
                give_copy(last - 2).wait_send()
                keep_copy(last - 2).wait()

            def halve(first, second):
                def body(r):
                    at = pl.ds(r, STRIP)
                    value = total[at]
                    first[last % 2, at] = value[:, :r_half]
                    second[last % 2, at] = value[:, r_half:]

                strips(chunk, body)

            @pl.when(depth == 0)
            def _():
                halve(keep, give)

            @pl.when(depth == 1)
            def _():
                halve(give, keep)

            give_copy(last).start()
            keep_copy(last).start()

        c2 = t - z
        p2 = c2 % 2

        @pl.when(live(c2))
        def _():
            for n in range(len(bits)):
                if n > 0:
                    bit_copy(n, c2).start()
                bit_copy(n, c2).wait()
                add_into_kept(p2, bit_in.at[n, p2])
            back_copy(c2).start()

        c1 = t - (z - 1)
        p1 = c1 % 2

        @pl.when(live(c1))
        def _():
            @pl.when(c1 == 0)
            def _():
                load_a.wait()

            for slot in range(z):

                def body(r):
                    h, l = split(ag[c1 % ring, slot, pl.ds(r, STRIP)])
                    at = pl.ds(pl.multiple_of(slot * chunk + r, STRIP), STRIP)
                    hi[at, :k_size] = h
                    lo[at, :k_size] = l

                strips(chunk, body)
            tile = tile_of(i_size)

            def body(j, carry):
                cols = pl.ds(pl.multiple_of(j * tile, tile), tile)
                prod[p1, :, cols] = product3(
                    hi[:, :k_size], lo[:, :k_size], a[:, cols], ((1,), (0,))
                )
                return carry

            lax.fori_loop(0, i_size // tile, body, 0)
            core_copy(c1).start()

        @pl.when(live(c2))
        def _():
            @pl.when(c2 == 0)
            def _():
                load_x.wait()

            back_copy(c2).wait()
            offset = depth * half + c2 * chunk
            here = offset // SLAB * PERIOD + offset % SLAB

            def residual(base, source):
                def body(r):
                    at = pl.multiple_of(base + r, STRIP)
                    value = source(r, at)
                    line = lax.broadcasted_iota(jnp.int32, value.shape, 0) + at
                    place = lax.broadcasted_iota(jnp.int32, value.shape, 1)
                    select = (line < chunk) & (place == here + line)
                    h, l = split(jnp.where(select, 2.0, 0.0) - value)
                    hi[pl.ds(at, STRIP), :i_size] = h
                    lo[pl.ds(at, STRIP), :i_size] = l

                strips(share, body)

            residual(core * share, lambda r, at: prod[p2, pl.ds(at, STRIP)])
            residual((1 - core) * share, lambda r, at: core_back[p2, pl.ds(r, STRIP)])
            tile = tile_of(x.shape[0])

            def body(j, carry):
                lines = pl.ds(pl.multiple_of(j * tile, tile), tile)
                value = product3(hi[:, :i_size], lo[:, :i_size], x[lines], ((1,), (1,)))
                part[c2 % z, :, :, lines] = value.reshape(z, chunk, tile)
                return carry

            lax.fori_loop(0, x.shape[0] // tile, body, 0)
            for way in range(2):

                @pl.when(places[way] == 0)
                def _():
                    rs_copy(way, 0, c2).start()

        @pl.when(live(c1))
        def _():
            core_copy(c1).wait()
            add_into_kept(p1, core_in.at[p1])
            bit_copy(0, c1).start()

        return carry

    lax.fori_loop(0, chunks + 2 * z - 1, step, 0)
    for c in range(chunks):
        give_copy(c).wait_recv()
        if c >= chunks - 2:
            give_copy(c).wait_send()
            keep_copy(c).wait()


def refresh(dims, w, covariance, iterate):
    row_count, z, chunk, chunks, ring, rs_ring = dims
    k_size, i_size = covariance.shape
    r_size = iterate.shape[0]
    n_bits = max(1, row_count.bit_length() - 2)
    group = z * chunk
    share = group // 2
    f32, bf16, dma = jnp.float32, jnp.bfloat16, pltpu.SemaphoreType.DMA
    anywhere = pl.BlockSpec(memory_space=pl.ANY)
    flops = 2 * 3 * 2 * group * chunks * k_size * i_size
    return pl.pallas_call(
        functools.partial(kernel, dims),
        out_shape=jax.ShapeDtypeStruct((2 * chunk * chunks, r_size // 2), f32),
        in_specs=[anywhere] * 3,
        out_specs=anywhere,
        scratch_shapes=[
            pltpu.VMEM((k_size, i_size), f32),
            pltpu.VMEM((r_size, i_size), f32),
            pltpu.VMEM((ring, z, chunk, k_size), f32),
            pltpu.VMEM((group, i_size if i_size >= k_size else k_size), bf16),
            pltpu.VMEM((group, i_size if i_size >= k_size else k_size), bf16),
            pltpu.VMEM((2, group, i_size), f32),
            pltpu.VMEM((2, share, i_size), f32),
            pltpu.VMEM((n_bits, 2, share, i_size), f32),
            pltpu.VMEM((2, share, i_size), f32),
            pltpu.VMEM((z, z, chunk, r_size), f32),
            pltpu.VMEM((rs_ring, 2, z - 1, chunk, r_size), f32),
            pltpu.VMEM((2, chunk, r_size // 2), f32),
            pltpu.VMEM((2, chunk, r_size // 2), f32),
            dma((2,)),
            dma((ring,)),
            dma((2, z - 1, ring)),
            dma((2, z - 1, ring)),
            dma((2,)),
            dma((2,)),
            dma((n_bits, 2)),
            dma((n_bits, 2)),
            dma((2,)),
            dma((2,)),
            dma((2, z - 1, rs_ring)),
            dma((2, z - 1, rs_ring)),
            dma((chunks,)),
            dma((chunks,)),
            dma((chunks,)),
        ],
        compiler_params=pltpu.CompilerParams(
            collective_id=0, has_side_effects=True, vmem_limit_bytes=VMEM_LIMIT
        ),
        cost_estimate=pl.CostEstimate(flops=flops, bytes_accessed=40000000, transcendentals=0),
    )(w, covariance, iterate)


VMEM_LIMIT = 65000000


def solution(mesh):
    row_count, z = mesh.shape["row"], mesh.shape["col"]

    def local(covariance, iterate):
        half = covariance.shape[1] // PERIOD * SLAB // 2
        chunk = min(CHUNK, half)
        chunks = half // chunk
        dims = (row_count, z, chunk, chunks, min(chunks, z + 1), min(chunks, z - 1))
        piece = min(half, SLAB)
        depth = lax.axis_index("depth")
        window = []
        for start in range(0, half, piece):
            near, far = column_of(start), column_of(half + start)
            window.append(
                jnp.where(
                    depth == 0,
                    iterate[:, near : near + piece],
                    iterate[:, far : far + piece],
                ).T
            )
        w = jnp.concatenate(window, axis=0)
        return refresh(dims, w, covariance, iterate).T

    in_specs = (P("row", "col"), P("row", "col"))
    out_specs = P(("row", "depth"), "col")
    return jax.shard_map(local, mesh=mesh, in_specs=in_specs, out_specs=out_specs, check_vma=False)
```

```python
import functools

import jax
import jax.numpy as jnp
from jax import lax
from jax.experimental import pallas as pl
from jax.experimental.pallas import tpu as pltpu
from jax.sharding import PartitionSpec as P

PERIOD = 896
SLAB = 512
CHUNK = 64
STRIP = 16
MESH = pl.DeviceIdType.MESH


def tile_of(size):
    return 256 if size % 256 == 0 else 128 if size % 128 == 0 else size


def split(value):
    hi = value.astype(jnp.bfloat16)
    return hi, (value - hi.astype(jnp.float32)).astype(jnp.bfloat16)


def product3(hi, lo, other, contract):
    b_hi, b_lo = split(other)
    dot = functools.partial(
        lax.dot_general,
        dimension_numbers=(contract, ((), ())),
        preferred_element_type=jnp.float32,
    )
    return dot(hi, b_hi) + (dot(lo, b_hi) + dot(hi, b_lo))


def strips(rows, body):
    def step(i, carry):
        body(pl.multiple_of(i * STRIP, STRIP))
        return carry

    lax.fori_loop(0, rows // STRIP, step, 0)


def kernel(
    dims, a_hbm, x_hbm, out, a, x, ag, hi, lo, prod, core_in, bit_in, core_back, part, rs,
    keep, give, load_sem, ag_send, ag_recv, core_send, core_recv, bit_send, bit_recv,
    back_send, back_recv, rs_send, rs_recv, give_send, give_recv, keep_sem,
):
    row_count, z, chunk, chunks, ring, rs_ring = dims
    row, col, depth = (lax.axis_index(n) for n in ("row", "col", "depth"))
    core = row % 2
    bits = [b for b in (2, 4, 8, 16, 32) if b < row_count]
    half = chunk * chunks
    group = z * chunk
    share = group // 2
    k_size, i_size = a.shape
    r_half = x.shape[0] // 2

    def partner(bit):
        return {"row": row + bit - 2 * bit * ((row // bit) % 2)}

    places = (col, z - 1 - col)
    targets = ({"col": col + 1}, {"col": col - 1})

    load_a = pltpu.make_async_copy(a_hbm, a, load_sem.at[0])
    load_x = pltpu.make_async_copy(x_hbm, x, load_sem.at[1])
    load_x.start()

    barrier = pltpu.get_barrier_semaphore()
    fixed = [partner(b) for b in [1] + bits] + [{"depth": 1 - depth}]
    for who in fixed:
        pl.semaphore_signal(barrier, inc=1, device_id=who, device_id_type=MESH)
    for way in range(2):

        @pl.when(places[way] < z - 1)
        def _():
            pl.semaphore_signal(barrier, inc=1, device_id=targets[way], device_id_type=MESH)

    ends = jnp.where(col == 0, 1, 0) + jnp.where(col == z - 1, 1, 0)
    pl.semaphore_wait(barrier, len(fixed) + 2 - ends)

    def remote(src, dst, send, recv, who):
        return pltpu.make_async_remote_copy(
            src_ref=src, dst_ref=dst, send_sem=send, recv_sem=recv,
            device_id=who, device_id_type=MESH,
        )

    def ag_copy(way, s, c):
        slot = c % ring
        came, lands = ((z - s) % z, z - 1 - s) if way == 0 else (s, s + 1)
        return remote(
            ag.at[slot, came], ag.at[slot, lands], ag_send.at[way, s, slot], ag_recv.at[way, s, slot],
            targets[way],
        )

    def rs_copy(way, s, c):
        slot = c % rs_ring
        src = part.at[c % z, z - 1 if way == 0 else 1] if s == 0 else rs.at[slot, way, s - 1]
        return remote(
            src, rs.at[slot, way, s], rs_send.at[way, s, slot], rs_recv.at[way, s, slot],
            targets[way],
        )

    mine = pl.ds(pl.multiple_of(core * share, share), share)
    theirs = pl.ds(pl.multiple_of((1 - core) * share, share), share)

    def core_copy(c):
        p = c % 2
        return remote(
            prod.at[p, theirs], core_in.at[p], core_send.at[p], core_recv.at[p], partner(1)
        )

    def back_copy(c):
        p = c % 2
        return remote(
            prod.at[p, mine], core_back.at[p], back_send.at[p], back_recv.at[p], partner(1)
        )

    def bit_copy(n, c):
        p = c % 2
        return remote(
            prod.at[p, mine], bit_in.at[n, p], bit_send.at[n, p], bit_recv.at[n, p],
            partner(bits[n]),
        )

    def give_copy(c):
        return remote(
            give.at[c % 2], out.at[pl.ds(depth * half + c * chunk, chunk)],
            give_send.at[c], give_recv.at[c], {"depth": 1 - depth},
        )

    def keep_copy(c):
        return pltpu.make_async_copy(
            keep.at[c % 2], out.at[pl.ds(depth * half + c * chunk, chunk)], keep_sem.at[c]
        )

    def live(c):
        return (c >= 0) & (c < chunks)

    def add_into_kept(p, other):
        base = core * share

        def body(r):
            at = pl.ds(pl.multiple_of(base + r, STRIP), STRIP)
            prod[p, at] = prod[p, at] + other[pl.ds(r, STRIP)]

        strips(share, body)

    load_x.wait()
    load_a.start()
    pair = min(chunks, max(1, 128 // chunk))

    def step(t, carry):
        for s in range(z - 1):
            c = t - 1 - s
            for way in range(2):
                place = places[way]

                @pl.when(live(c) & (place >= s + 1))
                def _():
                    ag_copy(way, s, c).wait_recv()

                @pl.when(live(c) & (place >= s) & (place < z - 1))
                def _():
                    ag_copy(way, s, c).wait_send()

        @pl.when((t % pair == 0) & (t < chunks))
        def _():
            offset = depth * half + t * chunk
            here = offset // SLAB * PERIOD + offset % SLAB
            block = x[:, pl.ds(pl.multiple_of(here, pair * chunk), pair * chunk)].T
            for n in range(pair):
                ag[(t + n) % ring, 0] = block[n * chunk : (n + 1) * chunk]

        for s in reversed(range(z - 1)):
            c = t - s
            for way in range(2):

                @pl.when(live(c) & (places[way] >= s) & (places[way] < z - 1))
                def _():
                    ag_copy(way, s, c).start()

        c2 = t - z
        p2 = c2 % 2

        c1 = t - (z - 1)
        p1 = c1 % 2

        @pl.when(live(c1))
        def _():
            @pl.when(c1 == 0)
            def _():
                load_a.wait()

            for slot in range(z):

                def body(r):
                    h, l = split(ag[c1 % ring, slot, pl.ds(r, STRIP)])
                    at = pl.ds(pl.multiple_of(slot * chunk + r, STRIP), STRIP)
                    hi[at, :k_size] = h
                    lo[at, :k_size] = l

                strips(chunk, body)
            tile = tile_of(i_size)

            def body(j, carry):
                cols = pl.ds(pl.multiple_of(j * tile, tile), tile)
                prod[p1, :, cols] = product3(
                    hi[:, :k_size], lo[:, :k_size], a[:, cols], ((1,), (0,))
                )
                return carry

            lax.fori_loop(0, i_size // tile, body, 0)
            core_copy(c1).start()

        @pl.when(live(c2))
        def _():
            for n in range(len(bits)):
                if n > 0:
                    bit_copy(n, c2).start()
                bit_copy(n, c2).wait()
                add_into_kept(p2, bit_in.at[n, p2])
            back_copy(c2).start()

        for s in range(z - 1):
            c = t - 1 - z - s
            for way in range(2):
                place = places[way]

                @pl.when(live(c) & (place >= 1) & (place <= s + 1))
                def _():
                    rs_copy(way, s, c).wait_recv()

                @pl.when(live(c) & (place <= s) & (place < z - 1))
                def _():
                    rs_copy(way, s, c).wait_send()

        for s in range(1, z - 1):
            c = t - z - s
            for way in range(2):
                place = places[way]
                slot = c % rs_ring
                term = part.at[c % z, z - 1 - s if way == 0 else s + 1]
                sum_ref = rs.at[slot, way, s - 1]

                @pl.when(live(c) & (place >= 1) & (place <= s) & (place < z - 1))
                def _():
                    def body(r):
                        at = pl.ds(r, STRIP)
                        sum_ref[at] = sum_ref[at] + term[at]

                    strips(chunk, body)

                @pl.when(live(c) & (place == 0))
                def _():
                    def body(r):
                        at = pl.ds(r, STRIP)
                        sum_ref[at] = term[at]

                    strips(chunk, body)

                @pl.when(live(c) & (place <= s) & (place < z - 1))
                def _():
                    rs_copy(way, s, c).start()

        last = t - (2 * z - 1)

        @pl.when(live(last))
        def _():
            total = part.at[last % z, 0]
            for way in range(2):

                @pl.when(places[way] > 0)
                def _():
                    def body(r):
                        at = pl.ds(r, STRIP)
                        total[at] = total[at] + rs[last % rs_ring, way, z - 2, at]

                    strips(chunk, body)

            @pl.when(last >= 2)
            def _():
                give_copy(last - 2).wait_send()
                keep_copy(last - 2).wait()

            def halve(first, second):
                def body(r):
                    at = pl.ds(r, STRIP)
                    value = total[at]
                    first[last % 2, at] = value[:, :r_half]
                    second[last % 2, at] = value[:, r_half:]

                strips(chunk, body)

            @pl.when(depth == 0)
            def _():
                halve(keep, give)

            @pl.when(depth == 1)
            def _():
                halve(give, keep)

            give_copy(last).start()
            keep_copy(last).start()

        @pl.when(live(c2))
        def _():
            back_copy(c2).wait()
            offset = depth * half + c2 * chunk
            here = offset // SLAB * PERIOD + offset % SLAB

            def residual(base, source):
                def body(r):
                    at = pl.multiple_of(base + r, STRIP)
                    value = source(r, at)
                    line = lax.broadcasted_iota(jnp.int32, value.shape, 0) + at
                    place = lax.broadcasted_iota(jnp.int32, value.shape, 1)
                    select = (line < chunk) & (place == here + line)
                    h, l = split(jnp.where(select, 2.0, 0.0) - value)
                    hi[pl.ds(at, STRIP), :i_size] = h
                    lo[pl.ds(at, STRIP), :i_size] = l

                strips(share, body)

            residual(core * share, lambda r, at: prod[p2, pl.ds(at, STRIP)])
            residual((1 - core) * share, lambda r, at: core_back[p2, pl.ds(r, STRIP)])

        @pl.when(live(c1))
        def _():
            core_copy(c1).wait()
            add_into_kept(p1, core_in.at[p1])
            bit_copy(0, c1).start()

        @pl.when(live(c2))
        def _():
            tile = tile_of(x.shape[0])

            def body(j, carry):
                lines = pl.ds(pl.multiple_of(j * tile, tile), tile)
                value = product3(hi[:, :i_size], lo[:, :i_size], x[lines], ((1,), (1,)))
                part[c2 % z, :, :, lines] = value.reshape(z, chunk, tile)
                return carry

            lax.fori_loop(0, x.shape[0] // tile, body, 0)
            for way in range(2):

                @pl.when(places[way] == 0)
                def _():
                    rs_copy(way, 0, c2).start()

        return carry

    lax.fori_loop(0, chunks + 2 * z - 1, step, 0)
    for c in range(chunks):
        give_copy(c).wait_recv()
        if c >= chunks - 2:
            give_copy(c).wait_send()
            keep_copy(c).wait()


def refresh(dims, covariance, iterate):
    row_count, z, chunk, chunks, ring, rs_ring = dims
    k_size, i_size = covariance.shape
    r_size = iterate.shape[0]
    n_bits = max(1, row_count.bit_length() - 2)
    group = z * chunk
    share = group // 2
    f32, bf16, dma = jnp.float32, jnp.bfloat16, pltpu.SemaphoreType.DMA
    anywhere = pl.BlockSpec(memory_space=pl.ANY)
    flops = 2 * 3 * 2 * group * chunks * k_size * i_size
    return pl.pallas_call(
        functools.partial(kernel, dims),
        out_shape=jax.ShapeDtypeStruct((2 * chunk * chunks, r_size // 2), f32),
        in_specs=[anywhere] * 2,
        out_specs=anywhere,
        scratch_shapes=[
            pltpu.VMEM((k_size, i_size), f32),
            pltpu.VMEM((r_size, i_size), f32),
            pltpu.VMEM((ring, z, chunk, k_size), f32),
            pltpu.VMEM((group, i_size if i_size >= k_size else k_size), bf16),
            pltpu.VMEM((group, i_size if i_size >= k_size else k_size), bf16),
            pltpu.VMEM((2, group, i_size), f32),
            pltpu.VMEM((2, share, i_size), f32),
            pltpu.VMEM((n_bits, 2, share, i_size), f32),
            pltpu.VMEM((2, share, i_size), f32),
            pltpu.VMEM((z, z, chunk, r_size), f32),
            pltpu.VMEM((rs_ring, 2, z - 1, chunk, r_size), f32),
            pltpu.VMEM((2, chunk, r_size // 2), f32),
            pltpu.VMEM((2, chunk, r_size // 2), f32),
            dma((2,)),
            dma((2, z - 1, ring)),
            dma((2, z - 1, ring)),
            dma((2,)),
            dma((2,)),
            dma((n_bits, 2)),
            dma((n_bits, 2)),
            dma((2,)),
            dma((2,)),
            dma((2, z - 1, rs_ring)),
            dma((2, z - 1, rs_ring)),
            dma((chunks,)),
            dma((chunks,)),
            dma((chunks,)),
        ],
        compiler_params=pltpu.CompilerParams(
            collective_id=0, has_side_effects=True, vmem_limit_bytes=VMEM_LIMIT
        ),
        cost_estimate=pl.CostEstimate(flops=flops, bytes_accessed=40000000, transcendentals=0),
    )(covariance, iterate)


VMEM_LIMIT = 65000000


def solution(mesh):
    row_count, z = mesh.shape["row"], mesh.shape["col"]

    def local(covariance, iterate):
        half = covariance.shape[1] // PERIOD * SLAB // 2
        chunk = min(CHUNK, half)
        chunks = half // chunk
        dims = (row_count, z, chunk, chunks, min(chunks, z + 1), min(chunks, z - 1))
        return refresh(dims, covariance, iterate).T

    in_specs = (P("row", "col"), P("row", "col"))
    out_specs = P(("row", "depth"), "col")
    return jax.shard_map(local, mesh=mesh, in_specs=in_specs, out_specs=out_specs, check_vma=False)
```

```python
import functools

import jax
import jax.numpy as jnp
from jax import lax
from jax.experimental import pallas as pl
from jax.experimental.pallas import tpu as pltpu
from jax.sharding import PartitionSpec as P

PERIOD = 896
SLAB = 512
CHUNK = 64
STRIP = 16
MESH = pl.DeviceIdType.MESH


def tile_of(size):
    return 256 if size % 256 == 0 else 128 if size % 128 == 0 else size


def split(value):
    hi = value.astype(jnp.bfloat16)
    return hi, (value - hi.astype(jnp.float32)).astype(jnp.bfloat16)


def product3(both, other, contract):
    b_hi, b_lo = split(other)
    dot = functools.partial(
        lax.dot_general,
        dimension_numbers=(contract, ((), ())),
        preferred_element_type=jnp.float32,
    )
    rows = both.shape[0] // 2
    first = dot(both, b_hi)
    return first[:rows] + (first[rows:] + dot(both[:rows], b_lo))


def strips(rows, body):
    def step(i, carry):
        body(pl.multiple_of(i * STRIP, STRIP))
        return carry

    lax.fori_loop(0, rows // STRIP, step, 0)


def kernel(
    dims, a_hbm, x_hbm, out, a, x, ag, both, prod, core_in, bit_in, core_back, part, rs,
    keep, give, load_sem, ag_send, ag_recv, core_send, core_recv, bit_send, bit_recv,
    back_send, back_recv, rs_send, rs_recv, give_send, give_recv, keep_sem,
):
    row_count, z, chunk, chunks, ring, rs_ring = dims
    row, col, depth = (lax.axis_index(n) for n in ("row", "col", "depth"))
    core = row % 2
    bits = [b for b in (2, 4, 8, 16, 32) if b < row_count]
    half = chunk * chunks
    group = z * chunk
    share = group // 2
    k_size, i_size = a.shape
    r_half = x.shape[0] // 2

    def partner(bit):
        return {"row": row + bit - 2 * bit * ((row // bit) % 2)}

    places = (col, z - 1 - col)
    targets = ({"col": col + 1}, {"col": col - 1})

    load_a = pltpu.make_async_copy(a_hbm, a, load_sem.at[0])
    load_x = pltpu.make_async_copy(x_hbm, x, load_sem.at[1])
    load_x.start()

    barrier = pltpu.get_barrier_semaphore()
    fixed = [partner(b) for b in [1] + bits] + [{"depth": 1 - depth}]
    for who in fixed:
        pl.semaphore_signal(barrier, inc=1, device_id=who, device_id_type=MESH)
    for way in range(2):

        @pl.when(places[way] < z - 1)
        def _():
            pl.semaphore_signal(barrier, inc=1, device_id=targets[way], device_id_type=MESH)

    ends = jnp.where(col == 0, 1, 0) + jnp.where(col == z - 1, 1, 0)
    pl.semaphore_wait(barrier, len(fixed) + 2 - ends)

    def remote(src, dst, send, recv, who):
        return pltpu.make_async_remote_copy(
            src_ref=src, dst_ref=dst, send_sem=send, recv_sem=recv,
            device_id=who, device_id_type=MESH,
        )

    def ag_copy(way, s, c):
        slot = c % ring
        came, lands = ((z - s) % z, z - 1 - s) if way == 0 else (s, s + 1)
        return remote(
            ag.at[slot, came], ag.at[slot, lands], ag_send.at[way, s, slot], ag_recv.at[way, s, slot],
            targets[way],
        )

    def rs_copy(way, s, c):
        slot = c % rs_ring
        src = part.at[c % z, z - 1 if way == 0 else 1] if s == 0 else rs.at[slot, way, s - 1]
        return remote(
            src, rs.at[slot, way, s], rs_send.at[way, s, slot], rs_recv.at[way, s, slot],
            targets[way],
        )

    mine = pl.ds(pl.multiple_of(core * share, share), share)
    theirs = pl.ds(pl.multiple_of((1 - core) * share, share), share)

    def core_copy(c):
        p = c % 2
        return remote(
            prod.at[p, theirs], core_in.at[p], core_send.at[p], core_recv.at[p], partner(1)
        )

    def back_copy(c):
        p = c % 2
        return remote(
            prod.at[p, mine], core_back.at[p], back_send.at[p], back_recv.at[p], partner(1)
        )

    def bit_copy(n, c):
        p = c % 2
        return remote(
            prod.at[p, mine], bit_in.at[n, p], bit_send.at[n, p], bit_recv.at[n, p],
            partner(bits[n]),
        )

    def give_copy(c):
        return remote(
            give.at[c % 2], out.at[pl.ds(depth * half + c * chunk, chunk)],
            give_send.at[c], give_recv.at[c], {"depth": 1 - depth},
        )

    def keep_copy(c):
        return pltpu.make_async_copy(
            keep.at[c % 2], out.at[pl.ds(depth * half + c * chunk, chunk)], keep_sem.at[c]
        )

    def live(c):
        return (c >= 0) & (c < chunks)

    def add_into_kept(p, other):
        base = core * share

        def body(r):
            at = pl.ds(pl.multiple_of(base + r, STRIP), STRIP)
            prod[p, at] = prod[p, at] + other[pl.ds(r, STRIP)]

        strips(share, body)

    load_x.wait()
    load_a.start()
    pair = min(chunks, max(1, 128 // chunk))

    def transfers(t, e):
        for s in range(z - 1):
            if (e - 1 - s) % 2:
                continue
            c = t + (e - 1 - s) // 2
            for way in range(2):
                place = places[way]

                @pl.when(live(c) & (place >= s + 1))
                def _():
                    ag_copy(way, s, c).wait_recv()

                @pl.when(live(c) & (place >= s) & (place < z - 1))
                def _():
                    ag_copy(way, s, c).wait_send()

        for s in reversed(range(z - 1)):
            if (e - s) % 2:
                continue
            c = t + (e - s) // 2
            for way in range(2):

                @pl.when(live(c) & (places[way] >= s) & (places[way] < z - 1))
                def _():
                    ag_copy(way, s, c).start()

        for s in range(z - 1):
            if (e - z - 4 - s) % 2:
                continue
            c = t + (e - z - 4 - s) // 2
            for way in range(2):
                place = places[way]

                @pl.when(live(c) & (place >= 1) & (place <= s + 1))
                def _():
                    rs_copy(way, s, c).wait_recv()

                @pl.when(live(c) & (place <= s) & (place < z - 1))
                def _():
                    rs_copy(way, s, c).wait_send()

        for s in range(1, z - 1):
            if (e - z - 3 - s) % 2:
                continue
            c = t + (e - z - 3 - s) // 2
            for way in range(2):
                place = places[way]
                slot = c % rs_ring
                term = part.at[c % z, z - 1 - s if way == 0 else s + 1]
                sum_ref = rs.at[slot, way, s - 1]

                @pl.when(live(c) & (place >= 1) & (place <= s) & (place < z - 1))
                def _():
                    def body(r):
                        at = pl.ds(r, STRIP)
                        sum_ref[at] = sum_ref[at] + term[at]

                    strips(chunk, body)

                @pl.when(live(c) & (place == 0))
                def _():
                    def body(r):
                        at = pl.ds(r, STRIP)
                        sum_ref[at] = term[at]

                    strips(chunk, body)

                @pl.when(live(c) & (place <= s) & (place < z - 1))
                def _():
                    rs_copy(way, s, c).start()

    def step(t, carry):
        @pl.when((t % pair == 0) & (t < chunks))
        def _():
            offset = depth * half + t * chunk
            here = offset // SLAB * PERIOD + offset % SLAB
            block = x[:, pl.ds(pl.multiple_of(here, pair * chunk), pair * chunk)].T
            for n in range(pair):
                ag[(t + n) % ring, 0] = block[n * chunk : (n + 1) * chunk]

        transfers(t, 0)

        last = t - z - 1

        @pl.when(live(last))
        def _():
            total = part.at[last % z, 0]
            for way in range(2):

                @pl.when(places[way] > 0)
                def _():
                    def body(r):
                        at = pl.ds(r, STRIP)
                        total[at] = total[at] + rs[last % rs_ring, way, z - 2, at]

                    strips(chunk, body)

            @pl.when(last >= 2)
            def _():
                give_copy(last - 2).wait_send()
                keep_copy(last - 2).wait()

            def halve(first, second):
                def body(r):
                    at = pl.ds(r, STRIP)
                    value = total[at]
                    first[last % 2, at] = value[:, :r_half]
                    second[last % 2, at] = value[:, r_half:]

                strips(chunk, body)

            @pl.when(depth == 0)
            def _():
                halve(keep, give)

            @pl.when(depth == 1)
            def _():
                halve(give, keep)

            give_copy(last).start()
            keep_copy(last).start()

        c2 = t - z // 2 - 1
        p2 = c2 % 2

        @pl.when(live(c2))
        def _():
            back_copy(c2).wait()
            offset = depth * half + c2 * chunk
            here = offset // SLAB * PERIOD + offset % SLAB

            def residual(base, source):
                def body(r):
                    at = pl.multiple_of(base + r, STRIP)
                    value = source(r, at)
                    line = lax.broadcasted_iota(jnp.int32, value.shape, 0) + at
                    place = lax.broadcasted_iota(jnp.int32, value.shape, 1)
                    select = (line < chunk) & (place == here + line)
                    h, l = split(jnp.where(select, 2.0, 0.0) - value)
                    both[pl.ds(at, STRIP), :i_size] = h
                    both[pl.ds(pl.multiple_of(group + at, STRIP), STRIP), :i_size] = l

                strips(share, body)

            residual(core * share, lambda r, at: prod[p2, pl.ds(at, STRIP)])
            residual((1 - core) * share, lambda r, at: core_back[p2, pl.ds(r, STRIP)])


        @pl.when(live(c2))
        def _():
            tile = tile_of(x.shape[0])

            def body(j, carry):
                lines = pl.ds(pl.multiple_of(j * tile, tile), tile)
                value = product3(both[:, :i_size], x[lines], ((1,), (1,)))
                part[c2 % z, :, :, lines] = value.reshape(z, chunk, tile)
                return carry

            lax.fori_loop(0, x.shape[0] // tile, body, 0)
            for way in range(2):

                @pl.when(places[way] == 0)
                def _():
                    rs_copy(way, 0, c2).start()

        transfers(t, 1)
        c1 = t - z // 2 + 1
        p1 = c1 % 2

        @pl.when(live(c1))
        def _():
            @pl.when(c1 == 0)
            def _():
                load_a.wait()

            for slot in range(z):

                def body(r):
                    h, l = split(ag[c1 % ring, slot, pl.ds(r, STRIP)])
                    at = pl.ds(pl.multiple_of(slot * chunk + r, STRIP), STRIP)
                    both[at, :k_size] = h
                    both[pl.ds(pl.multiple_of(group + slot * chunk + r, STRIP), STRIP), :k_size] = l

                strips(chunk, body)
            tile = tile_of(i_size)

            def body(j, carry):
                cols = pl.ds(pl.multiple_of(j * tile, tile), tile)
                prod[p1, :, cols] = product3(
                    both[:, :k_size], a[:, cols], ((1,), (0,))
                )
                return carry

            lax.fori_loop(0, i_size // tile, body, 0)
            core_copy(c1).start()

        cy = c1 - 1
        py = cy % 2

        @pl.when(live(cy))
        def _():
            for n in range(len(bits)):
                if n > 0:
                    bit_copy(n, cy).start()
                bit_copy(n, cy).wait()
                add_into_kept(py, bit_in.at[n, py])
            back_copy(cy).start()

        @pl.when(live(c1))
        def _():
            core_copy(c1).wait()
            add_into_kept(p1, core_in.at[p1])
            bit_copy(0, c1).start()

        return carry

    lax.fori_loop(0, chunks + z + 1, step, 0)
    for c in range(chunks):
        give_copy(c).wait_recv()
        if c >= chunks - 2:
            give_copy(c).wait_send()
            keep_copy(c).wait()


def refresh(dims, covariance, iterate):
    row_count, z, chunk, chunks, ring, rs_ring = dims
    k_size, i_size = covariance.shape
    r_size = iterate.shape[0]
    n_bits = max(1, row_count.bit_length() - 2)
    group = z * chunk
    share = group // 2
    f32, bf16, dma = jnp.float32, jnp.bfloat16, pltpu.SemaphoreType.DMA
    anywhere = pl.BlockSpec(memory_space=pl.ANY)
    flops = 2 * 3 * 2 * group * chunks * k_size * i_size
    return pl.pallas_call(
        functools.partial(kernel, dims),
        out_shape=jax.ShapeDtypeStruct((2 * chunk * chunks, r_size // 2), f32),
        in_specs=[anywhere] * 2,
        out_specs=anywhere,
        scratch_shapes=[
            pltpu.VMEM((k_size, i_size), f32),
            pltpu.VMEM((r_size, i_size), f32),
            pltpu.VMEM((ring, z, chunk, k_size), f32),
            pltpu.VMEM((2 * group, max(i_size, k_size)), bf16),
            pltpu.VMEM((2, group, i_size), f32),
            pltpu.VMEM((2, share, i_size), f32),
            pltpu.VMEM((n_bits, 2, share, i_size), f32),
            pltpu.VMEM((2, share, i_size), f32),
            pltpu.VMEM((z, z, chunk, r_size), f32),
            pltpu.VMEM((rs_ring, 2, z - 1, chunk, r_size), f32),
            pltpu.VMEM((2, chunk, r_size // 2), f32),
            pltpu.VMEM((2, chunk, r_size // 2), f32),
            dma((2,)),
            dma((2, z - 1, ring)),
            dma((2, z - 1, ring)),
            dma((2,)),
            dma((2,)),
            dma((n_bits, 2)),
            dma((n_bits, 2)),
            dma((2,)),
            dma((2,)),
            dma((2, z - 1, rs_ring)),
            dma((2, z - 1, rs_ring)),
            dma((chunks,)),
            dma((chunks,)),
            dma((chunks,)),
        ],
        compiler_params=pltpu.CompilerParams(
            collective_id=0, has_side_effects=True, vmem_limit_bytes=VMEM_LIMIT
        ),
        cost_estimate=pl.CostEstimate(flops=flops, bytes_accessed=40000000, transcendentals=0),
    )(covariance, iterate)


VMEM_LIMIT = 65000000


def solution(mesh):
    row_count, z = mesh.shape["row"], mesh.shape["col"]

    def local(covariance, iterate):
        half = covariance.shape[1] // PERIOD * SLAB // 2
        chunk = min(CHUNK, half)
        chunks = half // chunk
        dims = (row_count, z, chunk, chunks, min(chunks, z + 1), min(chunks, z - 1))
        return refresh(dims, covariance, iterate).T

    in_specs = (P("row", "col"), P("row", "col"))
    out_specs = P(("row", "depth"), "col")
    return jax.shard_map(local, mesh=mesh, in_specs=in_specs, out_specs=out_specs, check_vma=False)
```
